32 devices in a mesh: groups: 2 (over y), tensor: 4 (over z), adapter: 4 (over x, core).
Axes of the slice: x: 2, y: 2, z: 4, core: 2. Of those that a mesh axis runs over, the one named last changes fastest.
Arguments:
- attention_output: bfloat16 [4096, 8192], P(('groups', 'adapter'), 'tensor'), parts along dimension 0, may hold values from -6 to 6
- residual: bfloat16 [4096, 8192], P(('groups', 'adapter'), 'tensor'), parts along dimension 0, may hold values from -6 to 6
- output_projection_weight: bfloat16 [8192, 8192], P('tensor'), may hold values from -0.09375 to 0.09375
- adapter_down_weight: bfloat16 [16, 8192, 64], P(('tensor', 'adapter')), may hold values from -0.0625 to 0.0625
- adapter_up_weight: bfloat16 [16, 64, 8192], P(('tensor', 'adapter')), may hold values from -0.75 to 0.75
- request_adapter_index: int32 [4096, 1], P(('groups', 'adapter')), parts along dimension 0, may hold values from 0 to 15; in each aligned block of 512 rows (0 to 511, 512 to 1023, ...) at most 64 rows name the same one
- adapter_storage_index: int32 [16], replicated, may hold values from 0 to 15, each once
Outputs:
- mixed: bfloat16 [4096, 8192], P(('groups', 'adapter'), 'tensor'), parts along dimension 0
The draws below stay inside these ranges and needn't reach their ends.
There are 2 independent parts, one for each index of `groups`. The reference program is written for one: setup_inputs(seed, part) draws one part's arguments, and reference() takes and returns one part's arrays. A program takes and returns all parts, laid end to end along the dimension named above; an argument that names none is the same for every part. Nothing has to cross between parts.
Inputs may be any that keep to these rules, and one draw needn't show every extreme that they name: `request_adapter_index`: in each aligned block of 512 rows (the requests of one index of adapter) no id is named by more than 64 rows, a bound that some block reaches. `adapter_storage_index`: each index 0 to 15 appears once; index k is the device of combined index k along tensor+adapter, tensor slowest.
All inputs are finite; a program needn't handle non-finite values.
Results may differ from the reference program's by a relative error of at most 0.0039.
Values may be sent and summed in bfloat16 or wider, within the bound.
A program may use at most 192 MiB of HBM per device.

```python
import math
import jax
import jax.numpy as jnp
import numpy as np
from jax import lax

MODEL_WIDTH = 8192
ADAPTER_RANK = 64
ROWS_DEV = 512
TOKENS = 2048
ADAPTER_COUNT = 16
MOST = 64
N_ADAPTER = 4


def with_spikes(array, stream_key, source, target, blocks, factor):
    owner, partner = [(jnp.arange(array.shape[dim]) // (array.shape[dim] // blocks)).reshape([-1 if axis == dim else 1 for axis in range(array.ndim)]) for dim in (source, target)]
    chosen = jax.random.permutation(stream_key, blocks)[partner]
    strong = (owner == chosen) | (owner == (partner + blocks // 2) % blocks)
    return jnp.where(strong, factor * array, array)


def block_levels(key, shape, pieces, low, largest):
    def one(axis_at, blocks):
        draws = jax.random.uniform(jax.random.fold_in(jax.random.fold_in(key, 6), axis_at), (blocks,), jnp.float32, low / len(pieces), largest / len(pieces))
        return jnp.repeat(jnp.exp(draws), shape[axis_at] // blocks).reshape((-1,) + (1,) * (len(shape) - axis_at - 1))

    loudness = one(*pieces[0])
    for cut in pieces[1:]:
        loudness = loudness * one(*cut)
    return loudness


def shared_out(rng, own, number, rows, amount, top, reach, lean):
    sequence = jax.random.permutation(rng, amount)
    packed, ordinary = load_shares(amount, rows * top, reach, lean, True), load_shares(amount, rows * top, reach, lean, False)
    places = jnp.arange(amount)

    def named(tallies, offset_by):
        used = int((tallies > 0).sum())
        fixed = max(1, used // 4)
        shifted = fixed + (places - fixed + offset_by * (used - fixed)) % max(1, amount - fixed)
        return jnp.zeros((amount,), jnp.int32).at[sequence[jnp.where(places < fixed, places, shifted)]].set(jnp.asarray(tallies, jnp.int32))

    tallies = jnp.where(number % 4 == 0, named(packed, number // 4), named(ordinary, number - number // 4 - 1))
    mixed = jax.random.permutation(jax.random.fold_in(own, 3), amount)
    giver, receiver = mixed[0:amount // 2 * 2:2], mixed[1:amount // 2 * 2:2]
    slack = jnp.minimum(tallies[giver] - 1, reach - tallies[receiver]) // 2
    slack = jnp.where((giver == sequence[0]) | (receiver == sequence[0]) | (tallies[receiver] == 0), 0, jnp.maximum(slack, 0))
    shifted = jax.random.randint(jax.random.fold_in(own, 4), (amount // 2,), 0, 1 << 20) % (slack + 1)
    tallies = tallies.at[giver].add(-shifted).at[receiver].add(shifted)
    members = jnp.searchsorted(jnp.cumsum(tallies), jnp.arange(rows * top), side="right").astype(jnp.int32)
    table = members.reshape(top, rows).T
    table = table[jax.random.permutation(jax.random.fold_in(own, 1), rows)]
    offset_by = jax.random.randint(jax.random.fold_in(own, 2), (rows, 1), 0, top)
    return jnp.take_along_axis(table, (jnp.arange(top)[None, :] + offset_by) % top, axis=1)


def load_shares(amount, total, reach, slope, full):
    loads = [(1 << 20) // math.isqrt(grade ** slope) + 1 for grade in range(1, amount + 1)]
    largest = reach if full else min(reach, max(-(-total // amount), total * loads[0] // sum(loads)))
    least = 1 if total - largest >= amount - 1 else 0
    counts, rest = [largest] + [least] * (amount - 1), total - largest - least * (amount - 1)
    while rest > 0:
        candidates = [i for i in range(1, amount) if counts[i] < largest] or [i for i in range(1, amount) if counts[i] < reach]
        whole, budget = sum([loads[i] for i in candidates]), rest
        for i in candidates:
            extra = min(reach - counts[i], max(1, budget * loads[i] // whole), rest)
            counts[i] = counts[i] + extra
            rest = rest - extra
    return np.array(counts)


def centred(rng, dims, spread, limit, split=(), held_as=jnp.bfloat16):
    array = spread * jax.random.normal(rng, dims, jnp.float32)
    if split:
        array = array * block_levels(rng, dims, split, -0.22, 0.18)
    return jnp.clip(array, -limit, limit).astype(held_as)


def bell_draw_with(key, dims, width, limit, pieces, heavy, kind=jnp.bfloat16):
    drawn = width * jax.random.normal(key, dims, jnp.float32)
    if pieces:
        drawn = drawn * block_levels(key, dims, pieces, -0.22, 0.18)
    return jnp.clip(with_spikes(drawn, jax.random.fold_in(key, 3), *heavy), -limit, limit).astype(kind)


def setup_inputs(seed: int = 0, part: int = 0) -> dict:
    keys = jax.random.split(jax.random.key(seed), 8)
    own_keys = jax.random.split(jax.random.fold_in(keys[7], part), 8)
    attention_output = centred(own_keys[0], (TOKENS, MODEL_WIDTH), 1.0, 6.0, ((0, 4), (1, 4)))
    residual = centred(own_keys[1], (TOKENS, MODEL_WIDTH), 1.0, 6.0, ((0, 4), (1, 4)))
    output_projection_weight = bell_draw_with(keys[2], (MODEL_WIDTH, MODEL_WIDTH), MODEL_WIDTH ** -0.5, 0.09375, ((0, 4),), (0, 1, 4, 2.0))
    adapter_down_weight = centred(keys[3], (ADAPTER_COUNT, MODEL_WIDTH, ADAPTER_RANK), MODEL_WIDTH ** -0.5, 0.0625, ((0, 16),))
    adapter_up_weight = centred(keys[4], (ADAPTER_COUNT, ADAPTER_RANK, MODEL_WIDTH), ADAPTER_RANK ** -0.5, 0.75, ((0, 16),))
    request_adapter_index_keys = jax.random.split(jax.random.fold_in(own_keys[5], 1), TOKENS // ROWS_DEV)
    request_adapter_index_turns = jax.random.permutation(jax.random.fold_in(own_keys[5], 3), TOKENS // ROWS_DEV)
    request_adapter_index = jax.vmap(lambda own, number: shared_out(jax.random.fold_in(own_keys[5], 2), own, number, ROWS_DEV, ADAPTER_COUNT, 1, MOST, 2))(request_adapter_index_keys, request_adapter_index_turns).reshape((TOKENS, 1))
    adapter_storage_index = jax.random.permutation(keys[6], ADAPTER_COUNT).astype(jnp.int32)
    return {"attention_output": attention_output, "residual": residual, "output_projection_weight": output_projection_weight, "adapter_down_weight": adapter_down_weight, "adapter_up_weight": adapter_up_weight, "request_adapter_index": request_adapter_index, "adapter_storage_index": adapter_storage_index}


def reference(attention_output, residual, output_projection_weight, adapter_down_weight, adapter_up_weight, request_adapter_index, adapter_storage_index):
    slots = adapter_storage_index[request_adapter_index[:, 0]]
    base = jnp.dot(attention_output, output_projection_weight, preferred_element_type=jnp.float32)
    capacity = N_ADAPTER * MOST

    def one_adapter(delta, holder_device):
        picked = jnp.nonzero(slots == holder_device, size=capacity, fill_value=TOKENS)[0].astype(jnp.int32)
        selected_adapter = jnp.take(attention_output, picked, axis=0, mode="fill", fill_value=0)
        reduced_activation = jnp.dot(selected_adapter, adapter_down_weight[holder_device], preferred_element_type=jnp.float32).astype(jnp.bfloat16)
        adapter_update = jnp.dot(reduced_activation, adapter_up_weight[holder_device], preferred_element_type=jnp.float32).astype(jnp.bfloat16)
        delta = delta.at[picked].set(adapter_update, mode="drop")
        return delta, None

    delta, _ = lax.scan(one_adapter, jnp.zeros(attention_output.shape, jnp.bfloat16), jnp.arange(ADAPTER_COUNT, dtype=jnp.int32))
    total = residual.astype(jnp.float32) + base + delta.astype(jnp.float32)
    return total.astype(jnp.bfloat16)
```

```python
import jax
import jax.numpy as jnp
from jax import lax
from jax.sharding import PartitionSpec as P

CHUNKS = 4


def on_device(
    attention_output,
    residual,
    output_projection_weight,
    adapter_down_weight,
    adapter_up_weight,
    request_adapter_index,
    adapter_storage_index,
):
    rows, hidden = attention_output.shape
    n_tensor = lax.axis_size("tensor")
    n_adapter = lax.axis_size("adapter")
    owners = n_tensor * n_adapter
    rank = adapter_down_weight.shape[2]
    z = lax.axis_index("tensor")
    wire = jnp.bfloat16 if n_tensor <= 8 else jnp.float32

    down = adapter_down_weight[0].T.reshape(rank, n_tensor, hidden).transpose(1, 0, 2)
    up = adapter_up_weight[0].reshape(rank, n_tensor, hidden).transpose(1, 0, 2)
    pack = jnp.concatenate([down, up], axis=1)
    parts = [lax.dynamic_index_in_dim(pack, z, 0, keepdims=False)]
    for step in range(1, n_tensor):
        piece = lax.dynamic_index_in_dim(pack, (z + step) % n_tensor, 0, keepdims=False)
        pairs = [(i, (i + step) % n_tensor) for i in range(n_tensor)]
        parts.append(lax.ppermute(piece, "tensor", pairs))
    mine = jnp.stack(parts)
    every_down = lax.all_gather(mine[:, :rank], "adapter", axis=0, tiled=False)
    every_up = lax.all_gather(mine[:, rank:], "adapter", axis=0, tiled=False)
    every_down = every_down.reshape(owners * rank, hidden)
    every_up = every_up.reshape(owners * rank, hidden)

    labels = jnp.arange(owners, dtype=jnp.int32)
    named = request_adapter_index == labels[None, :]
    target = jnp.sum(jnp.where(named, adapter_storage_index[None, :], 0), axis=1)
    column = jnp.arange(owners * rank, dtype=jnp.int32) // rank
    source = (z - column % n_tensor + n_tensor) % n_tensor
    slot = source * n_adapter + column // n_tensor
    mask = target[:, None] == slot[None, :]

    wide = lax.dot_general(
        attention_output, every_down, (((1,), (1,)), ((), ())),
        preferred_element_type=jnp.float32,
    )
    wide = jnp.where(mask, wide, 0.0).reshape(rows, owners // 2, 2 * rank).sum(axis=1)
    shrunk = lax.psum(wide[:, :rank] + wide[:, rank:], "tensor").astype(jnp.bfloat16)
    spread = jnp.where(mask, jnp.tile(shrunk, (1, owners)), jnp.bfloat16(0))
    delta = jnp.dot(spread, every_up, preferred_element_type=jnp.float32).astype(jnp.bfloat16)

    width = hidden // CHUNKS
    ways = [1 if c % 2 == 0 else -1 for c in range(CHUNKS)]

    def term(block, c):
        start = block * hidden + c * width
        weight = lax.dynamic_slice_in_dim(output_projection_weight, start, width, 1)
        return jnp.dot(attention_output, weight, preferred_element_type=jnp.float32)

    sums = [None] * CHUNKS
    for step in range(n_tensor):
        for c in range(CHUNKS):
            way = ways[c]
            block = (z - way * (step + 1) + 2 * n_tensor) % n_tensor
            value = term(block, c)
            if step > 0:
                value = value + sums[c].astype(jnp.float32)
            if step < n_tensor - 1:
                pairs = [(i, (i + way) % n_tensor) for i in range(n_tensor)]
                value = lax.ppermute(value.astype(wire), "tensor", pairs)
            sums[c] = value
    base = jnp.concatenate(sums, axis=1)
    total = residual.astype(jnp.float32) + base + delta.astype(jnp.float32)
    return total.astype(jnp.bfloat16)


def solution(mesh):
    placed = (
        P(("groups", "adapter"), "tensor"),
        P(("groups", "adapter"), "tensor"),
        P("tensor", None),
        P(("tensor", "adapter"), None, None),
        P(("tensor", "adapter"), None, None),
        P(("groups", "adapter"), None),
        P(),
    )
    return jax.shard_map(
        on_device,
        mesh=mesh,
        in_specs=placed,
        out_specs=P(("groups", "adapter"), "tensor"),
        check_vma=False,
    )
```

```python
import jax
import jax.numpy as jnp
from jax import lax
from jax.sharding import PartitionSpec as P

CHUNKS = 4


def on_device(
    attention_output,
    residual,
    output_projection_weight,
    adapter_down_weight,
    adapter_up_weight,
    request_adapter_index,
    adapter_storage_index,
):
    rows, hidden = attention_output.shape
    n_tensor = lax.axis_size("tensor")
    n_adapter = lax.axis_size("adapter")
    owners = n_tensor * n_adapter
    rank = adapter_down_weight.shape[2]
    z = lax.axis_index("tensor")
    wire = jnp.bfloat16 if n_tensor <= 8 else jnp.float32

    width = hidden // CHUNKS
    ways = [1 if c % 2 == 0 else -1 for c in range(CHUNKS)]

    def term(block, c):
        start = block * hidden + c * width
        weight = lax.dynamic_slice_in_dim(output_projection_weight, start, width, 1)
        return jnp.dot(attention_output, weight, preferred_element_type=jnp.float32)

    def moved(value, way):
        pairs = [(i, (i + way) % n_tensor) for i in range(n_tensor)]
        return lax.ppermute(value, "tensor", pairs)

    first = [term((z - way + n_tensor) % n_tensor, c).astype(wire) for c, way in enumerate(ways)]
    sums = [moved(first[c], ways[c]) for c in range(CHUNKS)]

    adapter_down_weight, adapter_up_weight, _, _ = lax.optimization_barrier(
        (adapter_down_weight, adapter_up_weight, first[0], first[1])
    )
    down = adapter_down_weight[0].T.reshape(rank, n_tensor, hidden).transpose(1, 0, 2)
    up = adapter_up_weight[0].reshape(rank, n_tensor, hidden).transpose(1, 0, 2)
    pack = jnp.concatenate([down, up], axis=1)
    parts = [lax.dynamic_index_in_dim(pack, z, 0, keepdims=False)]
    for step in range(1, n_tensor):
        piece = lax.dynamic_index_in_dim(pack, (z + step) % n_tensor, 0, keepdims=False)
        pairs = [(i, (i + step) % n_tensor) for i in range(n_tensor)]
        parts.append(lax.ppermute(piece, "tensor", pairs))
    mine = jnp.stack(parts)
    every_down = lax.all_gather(mine[:, :rank], "adapter", axis=0, tiled=False)
    every_up = lax.all_gather(mine[:, rank:], "adapter", axis=0, tiled=False)
    every_down = every_down.reshape(owners * rank, hidden)
    every_up = every_up.reshape(owners * rank, hidden)

    labels = jnp.arange(owners, dtype=jnp.int32)
    named = request_adapter_index == labels[None, :]
    target = jnp.sum(jnp.where(named, adapter_storage_index[None, :], 0), axis=1)
    column = jnp.arange(owners * rank, dtype=jnp.int32) // rank
    source = (z - column % n_tensor + n_tensor) % n_tensor
    slot = source * n_adapter + column // n_tensor
    mask = target[:, None] == slot[None, :]

    wide = lax.dot_general(
        attention_output, every_down, (((1,), (1,)), ((), ())),
        preferred_element_type=jnp.float32,
    )
    wide = jnp.where(mask, wide, 0.0).reshape(rows, owners // 2, 2 * rank).sum(axis=1)
    share = wide[:, :rank] + wide[:, rank:]
    for step in range(1, n_tensor):
        values = []
        for c in range(CHUNKS):
            block = (z - ways[c] * (step + 1) + 2 * n_tensor) % n_tensor
            values.append(term(block, c) + sums[c].astype(jnp.float32))
        if step == n_tensor - 1:
            sums = values
            break
        values = [value.astype(wire) for value in values]
        if step == n_tensor - 2:
            *values, share = lax.optimization_barrier((*values, share))
        sums = [moved(values[c], ways[c]) for c in range(CHUNKS)]
    shares = lax.all_gather(share, "tensor", axis=0, tiled=False)
    shrunk = jnp.sum(shares, axis=0).astype(jnp.bfloat16)

    spread = jnp.where(mask, jnp.tile(shrunk, (1, owners)), jnp.bfloat16(0))
    delta = jnp.dot(spread, every_up, preferred_element_type=jnp.float32).astype(jnp.bfloat16)

    base = jnp.concatenate(sums, axis=1)
    total = residual.astype(jnp.float32) + base + delta.astype(jnp.float32)
    return total.astype(jnp.bfloat16)


def solution(mesh):
    placed = (
        P(("groups", "adapter"), "tensor"),
        P(("groups", "adapter"), "tensor"),
        P("tensor", None),
        P(("tensor", "adapter"), None, None),
        P(("tensor", "adapter"), None, None),
        P(("groups", "adapter"), None),
        P(),
    )
    return jax.shard_map(
        on_device,
        mesh=mesh,
        in_specs=placed,
        out_specs=P(("groups", "adapter"), "tensor"),
        check_vma=False,
    )
```

```python
import jax
import jax.numpy as jnp
from jax import lax
from jax.sharding import PartitionSpec as P

CHUNKS = 4


def on_device(
    attention_output,
    residual,
    output_projection_weight,
    adapter_down_weight,
    adapter_up_weight,
    request_adapter_index,
    adapter_storage_index,
):
    rows, hidden = attention_output.shape
    n_tensor = lax.axis_size("tensor")
    n_adapter = lax.axis_size("adapter")
    owners = n_tensor * n_adapter
    rank = adapter_down_weight.shape[2]
    z = lax.axis_index("tensor")
    wire = jnp.bfloat16 if n_tensor <= 8 else jnp.float32

    width = hidden // CHUNKS
    ways = [1 if c % 2 == 0 else -1 for c in range(CHUNKS)]

    def term(block, c):
        start = block * hidden + c * width
        weight = lax.dynamic_slice_in_dim(output_projection_weight, start, width, 1)
        return jnp.dot(attention_output, weight, preferred_element_type=jnp.float32)

    def moved(value, way):
        pairs = [(i, (i + way) % n_tensor) for i in range(n_tensor)]
        return lax.ppermute(value, "tensor", pairs)

    first = [term((z - way + n_tensor) % n_tensor, c).astype(wire) for c, way in enumerate(ways)]
    sums = [moved(first[c], ways[c]) for c in range(CHUNKS)]

    adapter_down_weight, adapter_up_weight, sums[0] = lax.optimization_barrier(
        (adapter_down_weight, adapter_up_weight, sums[0])
    )
    down = adapter_down_weight[0].T.reshape(rank, n_tensor, hidden).transpose(1, 0, 2)
    up = adapter_up_weight[0].reshape(rank, n_tensor, hidden).transpose(1, 0, 2)
    pack = jnp.concatenate([down, up], axis=1)
    parts = [lax.dynamic_index_in_dim(pack, z, 0, keepdims=False)]
    for step in range(1, n_tensor):
        piece = lax.dynamic_index_in_dim(pack, (z + step) % n_tensor, 0, keepdims=False)
        pairs = [(i, (i + step) % n_tensor) for i in range(n_tensor)]
        parts.append(lax.ppermute(piece, "tensor", pairs))
    mine = jnp.stack(parts)
    every_down = lax.all_gather(mine[:, :rank], "adapter", axis=0, tiled=False)
    every_up = lax.all_gather(mine[:, rank:], "adapter", axis=0, tiled=False)
    every_down = every_down.reshape(owners * rank, hidden)
    every_up = every_up.reshape(owners * rank, hidden)

    labels = jnp.arange(owners, dtype=jnp.int32)
    named = request_adapter_index == labels[None, :]
    target = jnp.sum(jnp.where(named, adapter_storage_index[None, :], 0), axis=1)
    column = jnp.arange(owners * rank, dtype=jnp.int32) // rank
    source = (z - column % n_tensor + n_tensor) % n_tensor
    slot = source * n_adapter + column // n_tensor
    mask = target[:, None] == slot[None, :]

    wide = lax.dot_general(
        attention_output, every_down, (((1,), (1,)), ((), ())),
        preferred_element_type=jnp.float32,
    )
    wide = jnp.where(mask, wide, 0.0).reshape(rows, owners // 2, 2 * rank).sum(axis=1)
    share = wide[:, :rank] + wide[:, rank:]
    for step in range(1, n_tensor):
        values = []
        for c in range(CHUNKS):
            block = (z - ways[c] * (step + 1) + 2 * n_tensor) % n_tensor
            values.append(term(block, c) + sums[c].astype(jnp.float32))
        if step == n_tensor - 1:
            sums = values
            break
        values = [value.astype(wire) for value in values]
        sums = [moved(values[c], ways[c]) for c in range(CHUNKS)]
    shrunk = lax.psum(share, "tensor").astype(jnp.bfloat16)

    spread = jnp.where(mask, jnp.tile(shrunk, (1, owners)), jnp.bfloat16(0))
    delta = jnp.dot(spread, every_up, preferred_element_type=jnp.float32).astype(jnp.bfloat16)

    base = jnp.concatenate(sums, axis=1)
    total = residual.astype(jnp.float32) + base + delta.astype(jnp.float32)
    return total.astype(jnp.bfloat16)


def solution(mesh):
    placed = (
        P(("groups", "adapter"), "tensor"),
        P(("groups", "adapter"), "tensor"),
        P("tensor", None),
        P(("tensor", "adapter"), None, None),
        P(("tensor", "adapter"), None, None),
        P(("groups", "adapter"), None),
        P(),
    )
    return jax.shard_map(
        on_device,
        mesh=mesh,
        in_specs=placed,
        out_specs=P(("groups", "adapter"), "tensor"),
        check_vma=False,
    )
```

```python
import jax
import jax.numpy as jnp
from jax import lax
from jax.sharding import PartitionSpec as P

CHUNKS = 4


def on_device(
    attention_output,
    residual,
    output_projection_weight,
    adapter_down_weight,
    adapter_up_weight,
    request_adapter_index,
    adapter_storage_index,
):
    rows, hidden = attention_output.shape
    n_tensor = lax.axis_size("tensor")
    n_adapter = lax.axis_size("adapter")
    owners = n_tensor * n_adapter
    rank = adapter_down_weight.shape[2]
    z = lax.axis_index("tensor")
    wire = jnp.bfloat16 if n_tensor <= 8 else jnp.float32

    width = hidden // CHUNKS
    ways = [1 if c % 2 == 0 else -1 for c in range(CHUNKS)]

    def term(block, c):
        start = block * hidden + c * width
        weight = lax.dynamic_slice_in_dim(output_projection_weight, start, width, 1)
        return jnp.dot(attention_output, weight, preferred_element_type=jnp.float32)

    def moved(value, way):
        pairs = [(i, (i + way) % n_tensor) for i in range(n_tensor)]
        return lax.ppermute(value, "tensor", pairs)

    first = [term((z - way + n_tensor) % n_tensor, c).astype(wire) for c, way in enumerate(ways)]
    sums = [moved(first[c], ways[c]) for c in range(CHUNKS)]

    adapter_down_weight, adapter_up_weight, _, _ = lax.optimization_barrier(
        (adapter_down_weight, adapter_up_weight, first[0], first[1])
    )
    down = adapter_down_weight[0].T.reshape(rank, n_tensor, hidden).transpose(1, 0, 2)
    up = adapter_up_weight[0].reshape(rank, n_tensor, hidden).transpose(1, 0, 2)
    pack = jnp.concatenate([down, up], axis=1)
    parts = [lax.dynamic_index_in_dim(pack, z, 0, keepdims=False)]
    for step in range(1, n_tensor):
        piece = lax.dynamic_index_in_dim(pack, (z + step) % n_tensor, 0, keepdims=False)
        pairs = [(i, (i + step) % n_tensor) for i in range(n_tensor)]
        parts.append(lax.ppermute(piece, "tensor", pairs))
    mine = jnp.stack(parts)
    every_down = lax.all_gather(mine[:, :rank], "adapter", axis=0, tiled=False)
    every_up = lax.all_gather(mine[:, rank:], "adapter", axis=0, tiled=False)
    every_down = every_down.reshape(owners * rank, hidden)
    every_up = every_up.reshape(owners * rank, hidden)

    labels = jnp.arange(owners, dtype=jnp.int32)
    named = request_adapter_index == labels[None, :]
    target = jnp.sum(jnp.where(named, adapter_storage_index[None, :], 0), axis=1)
    column = jnp.arange(owners * rank, dtype=jnp.int32) // rank
    source = (z - column % n_tensor + n_tensor) % n_tensor
    slot = source * n_adapter + column // n_tensor
    mask = target[:, None] == slot[None, :]

    wide = lax.dot_general(
        attention_output, every_down, (((1,), (1,)), ((), ())),
        preferred_element_type=jnp.float32,
    )
    wide = jnp.where(mask, wide, 0.0).reshape(rows, owners // 2, 2 * rank).sum(axis=1)
    share = wide[:, :rank] + wide[:, rank:]
    for step in range(1, n_tensor):
        values = []
        for c in range(CHUNKS):
            block = (z - ways[c] * (step + 1) + 2 * n_tensor) % n_tensor
            values.append(term(block, c) + sums[c].astype(jnp.float32))
        if step == n_tensor - 1:
            sums = values
            break
        values = [value.astype(wire) for value in values]
        if step == n_tensor - 2:
            *values, share = lax.optimization_barrier((*values, share))
        sums = [moved(values[c], ways[c]) for c in range(CHUNKS)]
    shrunk = lax.psum(share, "tensor").astype(jnp.bfloat16)

    spread = jnp.where(mask, jnp.tile(shrunk, (1, owners)), jnp.bfloat16(0))
    delta = jnp.dot(spread, every_up, preferred_element_type=jnp.float32).astype(jnp.bfloat16)

    base = jnp.concatenate(sums, axis=1)
    total = residual.astype(jnp.float32) + base + delta.astype(jnp.float32)
    return total.astype(jnp.bfloat16)


def solution(mesh):
    placed = (
        P(("groups", "adapter"), "tensor"),
        P(("groups", "adapter"), "tensor"),
        P("tensor", None),
        P(("tensor", "adapter"), None, None),
        P(("tensor", "adapter"), None, None),
        P(("groups", "adapter"), None),
        P(),
    )
    return jax.shard_map(
        on_device,
        mesh=mesh,
        in_specs=placed,
        out_specs=P(("groups", "adapter"), "tensor"),
        check_vma=False,
    )
```
